32 devices in a mesh: lat: 4 (over z), lyr: 4 (over x, core), dp: 2 (over y).
Axes of the slice: x: 2, y: 2, z: 4, core: 2. Of those that a mesh axis runs over, the one named last changes fastest.
Arguments:
- act_codes: bfloat16 [1024, 4, 4096], P('dp', 'lyr'), may hold values from -6 to 6
- act_scales: bfloat16 [1024, 4, 32], P('dp', 'lyr'), may hold values from 0.25 to 2.5
- latents: bfloat16 [1024, 16384], P('dp', 'lat'), may hold values from 0 to 36, as said below
- dec_weight: bfloat16 [16384, 4, 4096], P('lat', 'lyr', 'dp'), may hold values from -0.296875 to 0.296875
- dec_bias: float32 [4, 4096], P('lyr'), may hold values from -3 to 3
Outputs:
- grad_enc: float32 [4096, 4, 16384], P('dp', 'lyr', 'lat')
- grad_dec: float32 [16384, 4, 4096], P('lat', 'lyr', 'dp')
- grad_bias: float32 [16384], P('lat')
The draws below stay inside these ranges and needn't reach their ends.
Inputs may be any that keep to these rules, and one draw needn't show every extreme that they name: `latents`: nonnegative, with many exact zeros.
All inputs are finite; a program needn't handle non-finite values.
Results may differ from the reference program's by a relative error of at most 0.00065.
The reference program's roundings to bfloat16 on the way (of `inputs_bf`, `resid` and `grad_pre`) count: a program that leaves them out, or rounds other values in their place, can miss the bound.
Values may be sent and summed in bfloat16 or wider, within the bound.
No kernel may reach another device: no remote copies, remote signals or barrier semaphores. Data moves between devices by JAX's collectives and lax.ppermute only.
A program may use at most 384 MiB of HBM per device.

```python
import math
import jax
import jax.numpy as jnp
from jax import lax

D = 4096
LATENTS = 16384
LAYERS = 4
ROWS = 1024
BLOCKS = 32


def draw_latents(key, part):
    key = jax.random.fold_in(key, 5)
    k_base, k_rows, k_cols = jax.random.split(key, 3)
    raw_values = jnp.clip(jax.random.normal(k_base, (ROWS, LATENTS)), -4.0, 4.0)
    row_scale = jnp.exp(jax.random.uniform(k_rows, (ROWS, 1), minval=math.log(0.3), maxval=math.log(3.0)))
    col_scale = jnp.exp(jax.random.uniform(k_cols, (1, LATENTS), minval=math.log(0.3), maxval=math.log(3.0)))
    return (jnp.maximum(raw_values, 0.0) * row_scale * col_scale).astype(jnp.bfloat16)


def draw_dec_weight(key, part):
    key = jax.random.fold_in(key, 9)
    k_base, k_rows, k_cols = jax.random.split(key, 3)
    raw_values = jnp.clip(jax.random.normal(k_base, (LATENTS, LAYERS, D)), -4.0, 4.0)
    row_scale = jnp.exp(jax.random.uniform(k_rows, (LATENTS, LAYERS, 1), minval=math.log(0.3), maxval=math.log(3.0)))
    col_scale = jnp.exp(jax.random.uniform(k_cols, (1, 1, D), minval=math.log(0.3), maxval=math.log(3.0)))
    values = raw_values * row_scale * col_scale / math.sqrt(LATENTS)
    return jnp.clip(values, -0.296875, 0.296875).astype(jnp.bfloat16)


def block_scale(rng, shape, cuts, low, high):
    factor_of, own = 1.0, jax.random.fold_in(rng, 6)
    for position, shards_of in cuts:
        steps = jnp.exp(jax.random.uniform(jax.random.fold_in(own, position), (shards_of,), jnp.float32, low / len(cuts), high / len(cuts)))
        factor_of = factor_of * jnp.repeat(steps, shape[position] // shards_of).reshape([-1 if axis == position else 1 for axis in range(len(shape))])
    return factor_of


def gaussian(rng, shape, scale, bound, cuts=(), held_as=jnp.bfloat16):
    result = scale * jax.random.normal(rng, shape, jnp.float32)
    if cuts:
        result = result * block_scale(rng, shape, cuts, -0.22, 0.18)
    return jnp.clip(result, -bound, bound).astype(held_as)


def setup_inputs(seed: int = 0) -> dict:
    streams_of = jax.random.split(jax.random.key(seed), 6)
    act_codes = gaussian(streams_of[0], (ROWS, LAYERS, D), 1.0, 6.0, ((0, 2), (1, 4)))
    act_scales = jnp.clip(jnp.exp(math.log(2.5) - 2.3025851 * jax.random.uniform(streams_of[1], (ROWS, LAYERS, BLOCKS), jnp.float32) ** block_scale(streams_of[1], (ROWS, LAYERS, BLOCKS), ((0, 2), (1, 4)), -0.2, 0.2)), 0.25, 2.5).astype(jnp.bfloat16)
    latents = draw_latents(jax.random.fold_in(streams_of[5], 71), 0)
    dec_weight = draw_dec_weight(jax.random.fold_in(streams_of[5], 71), 0)
    dec_bias = gaussian(streams_of[4], (LAYERS, D), 0.5, 3.0, ((0, 4),), jnp.float32)
    return dict(act_codes=act_codes, act_scales=act_scales, latents=latents, dec_weight=dec_weight, dec_bias=dec_bias)


penalty = 1.0
epsilon = 1e-06

def dequantize(code_block, scale_block):
    row_count, layer_count, width = code_block.shape
    block_count = scale_block.shape[2]
    scaled = code_block.astype(jnp.float32).reshape(row_count, layer_count, block_count, width // block_count) * scale_block.astype(jnp.float32)[..., None]
    return scaled.reshape(row_count, layer_count, width)

def reference(act_codes, act_scales, latents, dec_weight, dec_bias):
    inputs = dequantize(act_codes, act_scales)
    inputs_bf = inputs.astype(jnp.bfloat16)
    norm_list = []
    resid_list = []
    grad_act = jnp.zeros((latents.shape[0], latents.shape[1]), jnp.float32)
    for layer in range(LAYERS):
        weight_layer = dec_weight[:, layer, :]
        wide = weight_layer.astype(jnp.float32)
        norm_list.append(jnp.sqrt(lax.optimization_barrier(jnp.sum(wide * wide, axis=1)) + epsilon))
        recon = jnp.dot(latents, weight_layer, preferred_element_type=jnp.float32)
        resid = (recon + dec_bias[layer][None, :] - inputs[:, layer, :]).astype(jnp.bfloat16)
        resid_list.append(resid)
        grad_act = grad_act + jnp.dot(resid, weight_layer.T, preferred_element_type=jnp.float32)
    row_norms = jnp.stack(norm_list, axis=1)
    norm_total = lax.optimization_barrier(jnp.sum(row_norms, axis=1))
    grad_act = grad_act + penalty * norm_total[None, :]
    grad_pre = jnp.where(latents > 0, grad_act, 0.0).astype(jnp.bfloat16)
    grad_bias = lax.optimization_barrier(jnp.sum(grad_pre.astype(jnp.float32), axis=0))
    act_sum = lax.optimization_barrier(jnp.sum(latents.astype(jnp.float32), axis=0))
    enc_list = []
    dec_list = []
    for layer in range(LAYERS):
        enc_list.append(jnp.dot(inputs_bf[:, layer, :].T, grad_pre, preferred_element_type=jnp.float32))
        scaled_rows = (penalty * act_sum / row_norms[:, layer])[:, None] * dec_weight[:, layer, :].astype(jnp.float32)
        dec_list.append(jnp.dot(latents.T, resid_list[layer], preferred_element_type=jnp.float32) + scaled_rows)
    grad_enc = jnp.stack(enc_list, axis=1)
    grad_dec = jnp.stack(dec_list, axis=1)
    return (grad_enc, grad_dec, grad_bias)
```

```python
import functools

import jax
import jax.numpy as jnp
from jax import lax
from jax.experimental import pallas as pl
from jax.experimental.pallas import tpu as pltpu
from jax.sharding import PartitionSpec as P

penalty = 1.0
epsilon = 1e-06

CHUNKS = 4
LANES = 128
TILE = 256
VMEM_BYTES = 44 * 1024 * 1024


def swap(value, axis, bit=1):
    size = lax.axis_size(axis)
    return lax.ppermute(value, axis, [(i, i ^ bit) for i in range(size)])


def swap_split(value, first_is_dp):
    n_lyr, n_dp = lax.axis_size("lyr"), lax.axis_size("dp")
    pairs = []
    for l in range(n_lyr):
        for p in range(n_dp):
            along_dp = (l % 2 == 0) == first_is_dp
            target = (l, p ^ 1) if along_dp else (l ^ 2, p)
            pairs.append((l * n_dp + p, target[0] * n_dp + target[1]))
    return lax.ppermute(value, ("lyr", "dp"), pairs)


def line_reduce(parts, me):
    n = parts.shape[0]

    def take(i):
        return lax.dynamic_index_in_dim(parts, jnp.clip(i, 0, n - 1), 0, keepdims=False)

    right = left = None
    for t in range(n - 1):
        to_right, to_left = take(n - 1 - t + me), take(t - (n - 1) + me)
        if t:
            to_right, to_left = to_right + right, to_left + left
        right = lax.ppermute(to_right, "lat", [(i, i + 1) for i in range(t + 1)])
        left = lax.ppermute(to_left, "lat", [(i, i - 1) for i in range(n - 1 - t, n)])
    return take(me) + right + left


def line_gather(block, me, n):
    rights, lefts = [], []
    to_right = to_left = block
    for t in range(n - 1):
        to_right = lax.ppermute(to_right, "lat", [(i, i + 1) for i in range(t, n - 1)])
        to_left = lax.ppermute(to_left, "lat", [(i, i - 1) for i in range(1, n - t)])
        rights.append(to_right)
        lefts.append(to_left)
    out = jnp.zeros((n,) + block.shape, block.dtype)
    out = lax.dynamic_update_index_in_dim(out, block, me, 0)
    for t in range(n - 1):
        got = jnp.where(me > t, rights[t], lefts[n - 2 - t])
        out = lax.dynamic_update_index_in_dim(out, got, lax.rem(me - 1 - t + n, n), 0)
    return out


def reduce_rows(partial, me):
    n = lax.axis_size("lat")
    rows, width = partial.shape
    if n <= 4:
        return line_reduce(partial.reshape(n, rows // n, width), me)
    return lax.psum_scatter(partial, "lat", scatter_dimension=0, tiled=True)


def gather_rows(block, me):
    n = lax.axis_size("lat")
    rows, width = block.shape
    if n <= 4:
        return line_gather(block, me, n).reshape(n * rows, width)
    return lax.all_gather(block, "lat", axis=0, tiled=True)


def store_rows(out_ref, value, first, count):
    rows = value.shape[0]
    for j in range(value.shape[1] // LANES):
        out_ref[pl.ds(first + j, rows, stride=count), :] = value[:, j * LANES : (j + 1) * LANES]


def dec_kernel(lat_ref, resid_ref, factor_ref, weight_ref, out_ref):
    width = resid_ref.shape[1]
    step = min(512, width)
    left = lat_ref[...].T
    for c in range(0, width, step):
        value = jnp.dot(left, resid_ref[:, c : c + step], preferred_element_type=jnp.float32)
        value = value + factor_ref[...] * weight_ref[:, c : c + step].astype(jnp.float32)
        store_rows(out_ref, value, c // LANES, width // LANES)


def enc_kernel(inputs_ref, grad_ref, out_ref):
    width = grad_ref.shape[1]
    step = min(512, width)
    left = inputs_ref[...].T
    for c in range(0, width, step):
        value = jnp.dot(left, grad_ref[:, c : c + step], preferred_element_type=jnp.float32)
        store_rows(out_ref, value, c // LANES, width // LANES)


def decoder_grad(lat, resid, factor, weight):
    rows, feats = lat.shape
    width = resid.shape[1]
    tile = min(TILE, feats)
    out = pl.pallas_call(
        dec_kernel,
        grid=(feats // tile,),
        in_specs=[
            pl.BlockSpec((rows, tile), lambda i: (0, i)),
            pl.BlockSpec((rows, width), lambda i: (0, 0)),
            pl.BlockSpec((tile, 1), lambda i: (i, 0)),
            pl.BlockSpec((tile, width), lambda i: (i, 0)),
        ],
        out_specs=pl.BlockSpec((tile * width // LANES, LANES), lambda i: (i, 0)),
        out_shape=jax.ShapeDtypeStruct((feats * width // LANES, LANES), jnp.float32),
        compiler_params=pltpu.CompilerParams(vmem_limit_bytes=VMEM_BYTES),
        cost_estimate=pl.CostEstimate(
            flops=2 * rows * feats * width,
            bytes_accessed=feats * width * 6 + rows * (feats + width) * 2,
            transcendentals=0,
        ),
    )(lat, resid, factor, weight)
    return out.reshape(feats, 1, width)


def encoder_grad(inputs, grad):
    rows, width = inputs.shape
    feats = grad.shape[1]
    tile = min(TILE, width)
    out = pl.pallas_call(
        enc_kernel,
        grid=(width // tile,),
        in_specs=[
            pl.BlockSpec((rows, tile), lambda i: (0, i)),
            pl.BlockSpec((rows, feats), lambda i: (0, 0)),
        ],
        out_specs=pl.BlockSpec((tile * feats // LANES, LANES), lambda i: (i, 0)),
        out_shape=jax.ShapeDtypeStruct((width * feats // LANES, LANES), jnp.float32),
        compiler_params=pltpu.CompilerParams(vmem_limit_bytes=VMEM_BYTES),
        cost_estimate=pl.CostEstimate(
            flops=2 * rows * feats * width,
            bytes_accessed=feats * width * 4 + rows * (feats + width) * 2,
            transcendentals=0,
        ),
    )(inputs, grad)
    return out.reshape(width, 1, feats)


def after(value, *events):
    return lax.optimization_barrier((value,) + events)[0]


def reduce_plane(partial, core, column):
    rows, feats = partial.shape
    sub = rows // 8
    blocks = partial.reshape(2, 2, 2, sub, feats)
    sent = lax.dynamic_index_in_dim(blocks, 1 - core, 2, keepdims=False)
    kept = lax.dynamic_index_in_dim(blocks, core, 2, keepdims=False)
    total = (kept + swap(sent, "lyr")).reshape(4, sub, feats)

    def pick(dp_other, column_other):
        index = 2 * dp_other + jnp.where(column_other == 1, 1 - column, column)
        return lax.dynamic_index_in_dim(total, index, 0, keepdims=False)

    first_dp, first_column = jnp.where(core == 0, 0, 1), jnp.where(core == 0, 1, 0)
    second_dp, second_column = first_column, first_dp
    got = swap_split(jnp.stack([pick(first_dp, first_column), pick(1, 1)]), False)
    mine = pick(0, 0) + got[0]
    later = pick(second_dp, second_column) + got[1]
    return mine + swap_split(later, True)


def gather_plane(mine, core, column):
    sub, feats = mine.shape
    second = swap_split(mine, True)
    pair = jnp.stack([mine, second])
    got = swap_split(pair, False)
    own_other = jnp.where(core == 0, got[0], second)
    other_own = jnp.where(core == 0, second, got[0])
    four = jnp.stack([jnp.stack([mine, own_other]), jnp.stack([other_own, got[1]])])
    four = jnp.where(column == 0, four, four[:, ::-1])
    twin = swap(four, "lyr")
    both = jnp.where(core == 0, jnp.stack([four, twin], 2), jnp.stack([twin, four], 2))
    return both.reshape(8 * sub, feats)


def shards(act_codes, act_scales, latents, dec_weight, dec_bias):
    me = lax.axis_index("lat")
    layer, half = lax.axis_index("lyr"), lax.axis_index("dp")
    core, column = layer % 2, layer // 2
    n_lat = lax.axis_size("lat")
    weight = dec_weight[:, 0, :]
    codes, scales = act_codes[:, 0, :], act_scales[:, 0, :]
    feats, width = weight.shape
    own_rows = latents.shape[0]
    piece = own_rows // CHUNKS
    block_count = scales.shape[1] // 2
    block_width = width // block_count
    spread = jnp.repeat(jnp.eye(block_count, dtype=jnp.bfloat16), block_width, axis=1)

    squares = jnp.sum(jnp.square(weight.astype(jnp.float32)), axis=1)
    squares = squares + swap(squares, "dp")
    row_norms = jnp.sqrt(squares + epsilon)
    bias = lax.dynamic_slice_in_dim(dec_bias, half * width, width, 1)

    def columns(value, which, count):
        return lax.dynamic_slice_in_dim(value, which * count, count, 1)

    scales_own = columns(scales, half, block_count)
    scales_other = swap(columns(scales, 1 - half, block_count), "dp")

    lat_chunks, inputs_chunks = [], []
    done = None
    for k in range(CHUNKS):
        span = slice(k * piece, (k + 1) * piece)
        own = latents[span]
        sent = lax.dynamic_slice_in_dim(own, core * (piece // 2), piece // 2, 0)
        sent_codes = columns(codes[span], 1 - half, width)
        if done is not None:
            sent, sent_codes = lax.optimization_barrier((sent, sent_codes, done))[:2]
        got = swap(sent, "dp")
        sent_codes = after(sent_codes, got)
        codes_other = swap(sent_codes, "dp")
        done = codes_other
        twin = swap(got, "lyr")
        other = jnp.where(core == 0, jnp.concatenate([got, twin]), jnp.concatenate([twin, got]))
        lat_chunks.append(jnp.concatenate([own, other]))
        code_rows = jnp.concatenate([columns(codes[span], half, width), codes_other])
        scale_rows = jnp.concatenate([scales_own[span], scales_other[span]])
        wide = jnp.dot(scale_rows, spread, preferred_element_type=jnp.float32)
        inputs_chunks.append(code_rows.astype(jnp.float32) * wide)

    resid_chunks, grad_chunks = [], []
    block = 2 * piece // n_lat
    last = None
    for k in range(CHUNKS):
        partial = jnp.dot(lat_chunks[k], weight, preferred_element_type=jnp.float32)
        recon = reduce_rows(partial, me)
        inputs = lax.dynamic_slice_in_dim(inputs_chunks[k], me * block, block, 0)
        resid = (recon + bias - inputs).astype(jnp.bfloat16)
        resid = gather_rows(resid, me)
        resid_chunks.append(resid)
        grad_part = lax.dot_general(
            resid, weight, (((1,), (1,)), ((), ())), preferred_element_type=jnp.float32
        )
        grad_part = grad_part + (0.5 * penalty) * row_norms[None, :]
        mine = reduce_plane(grad_part, core, column)
        sub = piece // 4
        lat_mine = lax.dynamic_slice_in_dim(latents, k * piece + layer * sub, sub, 0)
        grad_pre = jnp.where(lat_mine > 0, mine, 0.0).astype(jnp.bfloat16)
        grad_chunks.append(gather_plane(grad_pre, core, column))
        last = mine

    lat_all = jnp.concatenate(lat_chunks)
    inputs_bf = jnp.concatenate([x.astype(jnp.bfloat16) for x in inputs_chunks])
    act_sum = jnp.sum(lat_all.astype(jnp.float32), axis=0)
    factor = (penalty * act_sum / row_norms)[:, None]
    grad_dec = decoder_grad(lat_all, jnp.concatenate(resid_chunks), factor, weight)
    grad_all = jnp.concatenate(grad_chunks)
    grad_bias = jnp.sum(grad_all.astype(jnp.float32), axis=0)
    grad_enc = encoder_grad(inputs_bf, grad_all)
    return (grad_enc, grad_dec, grad_bias)


def solution(mesh):
    in_specs = (
        P("dp", "lyr", None),
        P("dp", "lyr", None),
        P("dp", "lat"),
        P("lat", "lyr", "dp"),
        P("lyr", None),
    )
    out_specs = (P("dp", "lyr", "lat"), P("lat", "lyr", "dp"), P("lat"))
    return jax.shard_map(shards, mesh=mesh, in_specs=in_specs, out_specs=out_specs, check_vma=False)
```

```python
import functools

import jax
import jax.numpy as jnp
from jax import lax
from jax.experimental import pallas as pl
from jax.experimental.pallas import tpu as pltpu
from jax.sharding import PartitionSpec as P

penalty = 1.0
epsilon = 1e-06

CHUNKS = (2, 3, 2, 1)
LANES = 128
TILE = 1024
GROUP = 8
VMEM_BYTES = 44 * 1024 * 1024


def swap(value, axis, bit=1):
    size = lax.axis_size(axis)
    return lax.ppermute(value, axis, [(i, i ^ bit) for i in range(size)])


def swap_split(value, first_is_dp):
    n_lyr, n_dp = lax.axis_size("lyr"), lax.axis_size("dp")
    pairs = []
    for l in range(n_lyr):
        for p in range(n_dp):
            along_dp = (l % 2 == 0) == first_is_dp
            target = (l, p ^ 1) if along_dp else (l ^ 2, p)
            pairs.append((l * n_dp + p, target[0] * n_dp + target[1]))
    return lax.ppermute(value, ("lyr", "dp"), pairs)


def reduce_rows(partial):
    return lax.psum_scatter(partial, "lat", scatter_dimension=0, tiled=True)


def gather_rows(block, me):
    n = lax.axis_size("lat")
    rows, width = block.shape
    if n > 4:
        return lax.all_gather(block, "lat", axis=0, tiled=True)
    out = jnp.zeros((n, rows, width), block.dtype)
    out = lax.dynamic_update_index_in_dim(out, block, me, 0)
    for shift in range(1, n):
        got = lax.ppermute(block, "lat", [(i, (i + shift) % n) for i in range(n)])
        out = lax.dynamic_update_index_in_dim(out, got, lax.rem(me - shift + n, n), 0)
    return out.reshape(n * rows, width)


def store_rows(out_ref, value):
    groups = value.shape[1] // LANES
    value = jnp.stack([value[:, j * LANES : (j + 1) * LANES] for j in range(groups)])
    out_ref[...] = jnp.swapaxes(value, 0, 1)


def product(lefts, rights):
    left = jnp.concatenate([ref[...] for ref in lefts], axis=1)
    right = jnp.concatenate([ref[...] for ref in rights], axis=0)
    return jnp.dot(left, right, preferred_element_type=jnp.float32)


def dec_kernel(count, *refs):
    factor_ref, weight_ref = refs[:2]
    lefts, rights, out_ref = refs[2 : 2 + count], refs[2 + count : 2 + 2 * count], refs[-1]
    value = product(lefts, rights)
    store_rows(out_ref, value + factor_ref[...] * weight_ref[...].astype(jnp.float32))


def enc_kernel(count, *refs):
    rights, (out_ref, bias_ref) = refs[1 : 1 + count], refs[1 + count :]
    store_rows(out_ref, product(refs[:1], rights))

    @pl.when(pl.program_id(1) == 0)
    def _():
        total = jnp.zeros(bias_ref.shape, jnp.float32)
        for ref in rights:
            total = total + jnp.sum(ref[...].astype(jnp.float32), axis=0, keepdims=True)
        bias_ref[...] = total


def params():
    return pltpu.CompilerParams(vmem_limit_bytes=VMEM_BYTES)


def decoder_grad(lefts, pieces, factor, weight, part, parts, earlier):
    feats, width = weight.shape
    rows = sum(piece.shape[0] for piece in pieces)
    share = feats // parts
    tile, step = min(TILE, share), min(GROUP * LANES, width)
    tiles = share // tile
    operands = [factor, weight, *lefts, *pieces]
    in_specs = [
        pl.BlockSpec((tile, 1), lambda i, j: (i + part * tiles, 0)),
        pl.BlockSpec((tile, step), lambda i, j: (i + part * tiles, j)),
    ]
    for left in lefts:
        in_specs.append(pl.BlockSpec((tile, left.shape[1]), lambda i, j: (i + part * tiles, 0)))
    for piece in pieces:
        in_specs.append(pl.BlockSpec((piece.shape[0], step), lambda i, j: (0, j)))
    aliases = {}
    if earlier is not None:
        aliases = {len(operands): 0}
        operands.append(earlier)
        in_specs.append(pl.BlockSpec(memory_space=pl.ANY))
    return pl.pallas_call(
        functools.partial(dec_kernel, len(pieces)),
        grid=(tiles, width // step),
        in_specs=in_specs,
        out_specs=pl.BlockSpec(
            (tile, step // LANES, LANES), lambda i, j: (i + part * tiles, j, 0)
        ),
        out_shape=jax.ShapeDtypeStruct((feats, width // LANES, LANES), jnp.float32),
        input_output_aliases=aliases,
        compiler_params=params(),
        cost_estimate=pl.CostEstimate(
            flops=2 * rows * share * width,
            bytes_accessed=share * width * 6 + rows * (share + width) * 2,
            transcendentals=0,
        ),
    )(*operands)


def encoder_grad(inputs_t, pieces):
    width, rows = inputs_t.shape
    feats = pieces[0].shape[1]
    tile, step = min(TILE, width), min(GROUP * LANES, feats)
    out, bias = pl.pallas_call(
        functools.partial(enc_kernel, len(pieces)),
        grid=(feats // step, width // tile),
        in_specs=[pl.BlockSpec((tile, rows), lambda j, i: (i, 0))]
        + [pl.BlockSpec((piece.shape[0], step), lambda j, i: (0, j)) for piece in pieces],
        out_specs=[
            pl.BlockSpec((tile, step // LANES, LANES), lambda j, i: (i, j, 0)),
            pl.BlockSpec((1, step), lambda j, i: (0, j)),
        ],
        out_shape=[
            jax.ShapeDtypeStruct((width, feats // LANES, LANES), jnp.float32),
            jax.ShapeDtypeStruct((1, feats), jnp.float32),
        ],
        compiler_params=params(),
        cost_estimate=pl.CostEstimate(
            flops=2 * rows * feats * width,
            bytes_accessed=feats * width * 4 + rows * (feats + width) * 2,
            transcendentals=0,
        ),
    )(inputs_t, *pieces)
    return out.reshape(width, 1, feats), bias.reshape(feats)


def after(value, *events):
    return lax.optimization_barrier((value,) + events)[0]


def transposed(value, selected):
    return lax.dot_general(
        value, selected, (((0,), (0,)), ((), ())), preferred_element_type=jnp.float32
    ).astype(jnp.bfloat16)


def reduce_plane(resid, weight, offset, core, column):
    sub, feats = resid.shape[0] // 8, weight.shape[0]
    terms = lax.dot_general(
        resid, weight, (((1,), (1,)), ((), ())), preferred_element_type=jnp.float32
    )
    blocks = (terms + offset[None, :]).reshape(2, 2, 2, sub, feats)
    to_send = lax.dynamic_index_in_dim(blocks, 1 - core, 2, keepdims=False)
    to_keep = lax.dynamic_index_in_dim(blocks, core, 2, keepdims=False)
    total = (to_keep + swap(to_send, "lyr")).reshape(4, sub, feats)

    def pick(dp_other, column_other):
        index = 2 * dp_other + jnp.where(column_other == 1, 1 - column, column)
        return lax.dynamic_index_in_dim(total, index, 0, keepdims=False)

    first_dp, first_column = jnp.where(core == 0, 0, 1), jnp.where(core == 0, 1, 0)
    second_dp, second_column = first_column, first_dp
    got = swap_split(jnp.stack([pick(first_dp, first_column), pick(1, 1)]), False)
    mine = pick(0, 0) + got[0]
    later = pick(second_dp, second_column) + got[1]
    return total, mine + swap_split(later, True)


def gather_plane(mine):
    pair = jnp.stack([mine, swap_split(mine, True)])
    twin_pair = swap(pair, "lyr")
    got = swap_split(pair, False)
    twin_got = swap(got, "lyr")
    rows = jnp.concatenate([pair, got, twin_pair, twin_got])
    return rows.reshape(-1, mine.shape[1]), pair


def plane_rows(core, column):
    order = []
    for c in (core, 1 - core):
        across, beside = 4 + 2 * column + c, 2 * (1 - column) + c
        order += [
            2 * column + c,
            jnp.where(c == 0, across, beside),
            jnp.where(c == 0, beside, across),
            4 + 2 * (1 - column) + c,
        ]
    return jnp.stack(order)


def shards(act_codes, act_scales, latents, dec_weight, dec_bias):
    me = lax.axis_index("lat")
    layer, half = lax.axis_index("lyr"), lax.axis_index("dp")
    core, column = layer % 2, layer // 2
    n_lat = lax.axis_size("lat")
    weight = dec_weight[:, 0, :]
    codes, scales = act_codes[:, 0, :], act_scales[:, 0, :]
    feats, width = weight.shape
    own_rows = latents.shape[0]
    unit = own_rows // sum(CHUNKS)
    starts = [unit * sum(CHUNKS[:k]) for k in range(len(CHUNKS) + 1)]
    block_count = scales.shape[1] // 2
    spread = jnp.repeat(jnp.eye(block_count, dtype=jnp.bfloat16), width // block_count, axis=1)

    def columns(value, which, count):
        return lax.dynamic_slice_in_dim(value, which * count, count, 1)

    groups = [(0, 1), (1, 2), (2, len(CHUNKS))]
    lat_chunks, codes_other = [], []
    partials, recons, resid_own, resid_chunks, grad_chunks, mines = [], [], [], [], [], []

    def local_recon(k):
        lat = lat_chunks[k] if k < 2 else after(lat_chunks[k], resid_own[k - 2])
        partials.append(jnp.dot(lat, weight, preferred_element_type=jnp.float32))
        recons.append(reduce_rows(after(partials[k], *recons[2:k])))

    done = None
    for first, last in groups:
        rows = starts[last] - starts[first]
        source = latents if done is None else after(latents, done)
        sent = lax.dynamic_slice_in_dim(source, starts[first] + core * (rows // 2), rows // 2, 0)
        got = swap(sent, "dp")
        done = got
        if partials:
            got = after(got, partials[-1])
        twin = swap(got, "lyr")
        both = jnp.where(core == 0, jnp.stack([got, twin]), jnp.stack([twin, got]))
        both = both.reshape(rows, feats)
        for k in range(first, last):
            inner = slice(starts[k] - starts[first], starts[k + 1] - starts[first])
            lat_chunks.append(jnp.concatenate([latents[starts[k] : starts[k + 1]], both[inner]]))
        if len(partials) < 2:
            local_recon(first)
        codes_here = after(codes, *partials[first : first + 1], done)
        span = slice(starts[first], starts[last])
        codes_got = swap(columns(codes_here[span], 1 - half, width), "dp")
        for k in range(first, last):
            inner = slice(starts[k] - starts[first], starts[k + 1] - starts[first])
            codes_other.append(codes_got[inner])

    scales_here = after(scales, partials[0])
    weight_here = after(weight, partials[0])
    scales_own = columns(scales_here, half, block_count)
    scales_other = swap(columns(scales_here, 1 - half, block_count), "dp")
    squares = jnp.sum(jnp.square(weight_here.astype(jnp.float32)), axis=1)
    squares = squares + swap(squares, "dp")
    row_norms = jnp.sqrt(squares + epsilon)
    offset = (0.5 * penalty) * row_norms
    bias = lax.dynamic_slice_in_dim(dec_bias, half * width, width, 1)

    inputs_chunks = []
    for k in range(len(CHUNKS)):
        span = slice(starts[k], starts[k + 1])
        code_rows = jnp.concatenate([columns(codes[span], half, width), codes_other[k]])
        scale_rows = jnp.concatenate([scales_own[span], scales_other[span]])
        wide = jnp.dot(scale_rows, spread, preferred_element_type=jnp.float32)
        inputs_chunks.append(code_rows.astype(jnp.float32) * wide)
    count = len(CHUNKS)
    for k in range(count):
        if len(partials) < min(k + 2, count):
            local_recon(k + 1)
        events = partials[k + 1 : k + 2]
        if 2 <= k < count - 1:
            events = events + [mines[k - 2]]
        recon = after(recons[k], *events) if events else recons[k]
        block = 2 * (starts[k + 1] - starts[k]) // n_lat
        inputs = lax.dynamic_slice_in_dim(inputs_chunks[k], me * block, block, 0)
        resid_own.append((recon + bias - inputs).astype(jnp.bfloat16))
        resid = gather_rows(resid_own[k], me)
        resid_chunks.append(resid)
        if k >= 1:
            resid = after(resid, mines[k - 1])
        total, mine = reduce_plane(resid, weight, offset, core, column)
        if k >= 1:
            mine = after(mine, grad_chunks[k - 1])
        mines.append(mine)
        sub = (starts[k + 1] - starts[k]) // 4
        lat_mine = lax.dynamic_slice_in_dim(latents, starts[k] + layer * sub, sub, 0)
        grad_pre = jnp.where(lat_mine > 0, mine, 0.0).astype(jnp.bfloat16)
        grad_rows, pair = gather_plane(grad_pre)
        grad_chunks.append(grad_rows)

    inputs_bf = jnp.concatenate([x.astype(jnp.bfloat16) for x in inputs_chunks])
    order = after(plane_rows(core, column), resid_own[0])
    sources = []
    for k in range(count):
        sub = (starts[k + 1] - starts[k]) // 4
        source = (order * sub)[:, None] + jnp.arange(sub)[None, :]
        sources.append(2 * starts[k] + source.reshape(-1))
    rows = jnp.arange(2 * own_rows)
    selected = (rows[:, None] == jnp.concatenate(sources)[None, :]).astype(jnp.bfloat16)
    inputs_t = transposed(inputs_bf, selected)

    lat_t, act_sum = [], 0.0
    for k in range(count):
        lat = after(lat_chunks[k], resid_own[min(max(k, 1), 2)])
        lat_t.append(transposed(lat, jnp.eye(lat.shape[0], dtype=jnp.bfloat16)))
        act_sum = act_sum + jnp.sum(lat.astype(jnp.float32), axis=0)
    factor = (penalty * act_sum / row_norms)[:, None]

    grad_dec = None
    for part, event in enumerate((total, mine)):
        pieces = [after(lat_t[0], event)] + lat_t[1:]
        grad_dec = decoder_grad(pieces, resid_chunks, factor, weight, part, 2, grad_dec)
    grad_enc, grad_bias = encoder_grad(inputs_t, grad_chunks)
    return (grad_enc, grad_dec.reshape(feats, 1, width), grad_bias)


def solution(mesh):
    in_specs = (
        P("dp", "lyr", None),
        P("dp", "lyr", None),
        P("dp", "lat"),
        P("lat", "lyr", "dp"),
        P("lyr", None),
    )
    out_specs = (P("dp", "lyr", "lat"), P("lat", "lyr", "dp"), P("lat"))
    return jax.shard_map(shards, mesh=mesh, in_specs=in_specs, out_specs=out_specs, check_vma=False)
```

```python
import functools

import jax
import jax.numpy as jnp
from jax import lax
from jax.experimental import pallas as pl
from jax.experimental.pallas import tpu as pltpu
from jax.sharding import PartitionSpec as P

penalty = 1.0
epsilon = 1e-06

CHUNKS = (3, 3, 2)
LANES = 128
TILE = 1024
GROUP = 8
VMEM_BYTES = 44 * 1024 * 1024


def swap(value, axis, bit=1):
    size = lax.axis_size(axis)
    return lax.ppermute(value, axis, [(i, i ^ bit) for i in range(size)])


def swap_split(value, first_is_dp):
    n_lyr, n_dp = lax.axis_size("lyr"), lax.axis_size("dp")
    pairs = []
    for l in range(n_lyr):
        for p in range(n_dp):
            along_dp = (l % 2 == 0) == first_is_dp
            target = (l, p ^ 1) if along_dp else (l ^ 2, p)
            pairs.append((l * n_dp + p, target[0] * n_dp + target[1]))
    return lax.ppermute(value, ("lyr", "dp"), pairs)


def reduce_rows(partial):
    return lax.psum_scatter(partial, "lat", scatter_dimension=0, tiled=True)


def gather_rows(block, me):
    n = lax.axis_size("lat")
    rows, width = block.shape
    if n > 4:
        return lax.all_gather(block, "lat", axis=0, tiled=True)
    out = jnp.zeros((n, rows, width), block.dtype)
    out = lax.dynamic_update_index_in_dim(out, block, me, 0)
    for shift in sorted(range(1, n), key=lambda i: min(i, n - i)):
        got = lax.ppermute(block, "lat", [(i, (i + shift) % n) for i in range(n)])
        out = lax.dynamic_update_index_in_dim(out, got, lax.rem(me - shift + n, n), 0)
    return out.reshape(n * rows, width)


def store_rows(out_ref, value):
    groups = value.shape[1] // LANES
    value = jnp.stack([value[:, j * LANES : (j + 1) * LANES] for j in range(groups)])
    out_ref[...] = jnp.swapaxes(value, 0, 1)


def product(lefts, rights):
    left = jnp.concatenate([ref[...] for ref in lefts], axis=1)
    right = jnp.concatenate([ref[...] for ref in rights], axis=0)
    return jnp.dot(left, right, preferred_element_type=jnp.float32)


def dec_kernel(count, *refs):
    factor_ref, weight_ref = refs[:2]
    lefts, rights, out_ref = refs[2 : 2 + count], refs[2 + count : 2 + 2 * count], refs[-1]
    value = product(lefts, rights)
    store_rows(out_ref, value + factor_ref[...] * weight_ref[...].astype(jnp.float32))


def enc_kernel(count, *refs):
    rights, (out_ref, bias_ref) = refs[1 : 1 + count], refs[1 + count :]
    store_rows(out_ref, product(refs[:1], rights))

    @pl.when(pl.program_id(1) == 0)
    def _():
        total = jnp.zeros(bias_ref.shape, jnp.float32)
        for ref in rights:
            total = total + jnp.sum(ref[...].astype(jnp.float32), axis=0, keepdims=True)
        bias_ref[...] = total


def params():
    return pltpu.CompilerParams(vmem_limit_bytes=VMEM_BYTES)


def decoder_grad(lefts, pieces, factor, weight, part, parts, earlier):
    feats, width = weight.shape
    rows = sum(piece.shape[0] for piece in pieces)
    share = feats // parts
    tile, step = min(TILE, share), min(GROUP * LANES, width)
    tiles = share // tile
    operands = [factor, weight, *lefts, *pieces]
    in_specs = [
        pl.BlockSpec((tile, 1), lambda i, j: (i + part * tiles, 0)),
        pl.BlockSpec((tile, step), lambda i, j: (i + part * tiles, j)),
    ]
    for left in lefts:
        in_specs.append(pl.BlockSpec((tile, left.shape[1]), lambda i, j: (i + part * tiles, 0)))
    for piece in pieces:
        in_specs.append(pl.BlockSpec((piece.shape[0], step), lambda i, j: (0, j)))
    aliases = {}
    if earlier is not None:
        aliases = {len(operands): 0}
        operands.append(earlier)
        in_specs.append(pl.BlockSpec(memory_space=pl.ANY))
    return pl.pallas_call(
        functools.partial(dec_kernel, len(pieces)),
        grid=(tiles, width // step),
        in_specs=in_specs,
        out_specs=pl.BlockSpec(
            (tile, step // LANES, LANES), lambda i, j: (i + part * tiles, j, 0)
        ),
        out_shape=jax.ShapeDtypeStruct((feats, width // LANES, LANES), jnp.float32),
        input_output_aliases=aliases,
        compiler_params=params(),
        cost_estimate=pl.CostEstimate(
            flops=2 * rows * share * width,
            bytes_accessed=share * width * 6 + rows * (share + width) * 2,
            transcendentals=0,
        ),
    )(*operands)


def encoder_grad(inputs_t, pieces):
    width, rows = inputs_t.shape
    feats = pieces[0].shape[1]
    tile, step = min(TILE, width), min(GROUP * LANES, feats)
    out, bias = pl.pallas_call(
        functools.partial(enc_kernel, len(pieces)),
        grid=(feats // step, width // tile),
        in_specs=[pl.BlockSpec((tile, rows), lambda j, i: (i, 0))]
        + [pl.BlockSpec((piece.shape[0], step), lambda j, i: (0, j)) for piece in pieces],
        out_specs=[
            pl.BlockSpec((tile, step // LANES, LANES), lambda j, i: (i, j, 0)),
            pl.BlockSpec((1, step), lambda j, i: (0, j)),
        ],
        out_shape=[
            jax.ShapeDtypeStruct((width, feats // LANES, LANES), jnp.float32),
            jax.ShapeDtypeStruct((1, feats), jnp.float32),
        ],
        compiler_params=params(),
        cost_estimate=pl.CostEstimate(
            flops=2 * rows * feats * width,
            bytes_accessed=feats * width * 4 + rows * (feats + width) * 2,
            transcendentals=0,
        ),
    )(inputs_t, *pieces)
    return out.reshape(width, 1, feats), bias.reshape(feats)


def after(value, *events):
    return lax.optimization_barrier((value,) + events)[0]


def transposed(value, selected):
    return lax.dot_general(
        value, selected, (((0,), (0,)), ((), ())), preferred_element_type=jnp.float32
    ).astype(jnp.bfloat16)


def reduce_pair(resid, weight, offset, core):
    sub, feats = resid.shape[0] // 8, weight.shape[0]
    terms = lax.dot_general(
        resid, weight, (((1,), (1,)), ((), ())), preferred_element_type=jnp.float32
    )
    blocks = (terms + offset[None, :]).reshape(2, 2, 2, sub, feats)
    to_send = lax.dynamic_index_in_dim(blocks, 1 - core, 2, keepdims=False)
    to_keep = lax.dynamic_index_in_dim(blocks, core, 2, keepdims=False)
    return (to_keep + swap(to_send, "lyr")).reshape(4, sub, feats), to_send


def reduce_plane(total, core, column):
    def pick(dp_other, column_other):
        index = 2 * dp_other + jnp.where(column_other == 1, 1 - column, column)
        return lax.dynamic_index_in_dim(total, index, 0, keepdims=False)

    first_dp, first_column = jnp.where(core == 0, 0, 1), jnp.where(core == 0, 1, 0)
    second_dp, second_column = first_column, first_dp
    got = swap_split(jnp.stack([pick(first_dp, first_column), pick(1, 1)]), False)
    mine = pick(0, 0) + got[0]
    later = pick(second_dp, second_column) + got[1]
    return mine + swap_split(later, True)


def gather_plane(mine):
    pair = jnp.stack([mine, swap_split(mine, True)])
    twin_pair = swap(pair, "lyr")
    got = swap_split(pair, False)
    twin_got = swap(got, "lyr")
    rows = jnp.concatenate([pair, got, twin_pair, twin_got])
    return rows.reshape(-1, mine.shape[1]), pair


def plane_rows(core, column):
    order = []
    for c in (core, 1 - core):
        across, beside = 4 + 2 * column + c, 2 * (1 - column) + c
        order += [
            2 * column + c,
            jnp.where(c == 0, across, beside),
            jnp.where(c == 0, beside, across),
            4 + 2 * (1 - column) + c,
        ]
    return jnp.stack(order)


def shards(act_codes, act_scales, latents, dec_weight, dec_bias):
    me = lax.axis_index("lat")
    layer, half = lax.axis_index("lyr"), lax.axis_index("dp")
    core, column = layer % 2, layer // 2
    n_lat = lax.axis_size("lat")
    weight = dec_weight[:, 0, :]
    codes, scales = act_codes[:, 0, :], act_scales[:, 0, :]
    feats, width = weight.shape
    own_rows = latents.shape[0]
    unit = own_rows // sum(CHUNKS)
    starts = [unit * sum(CHUNKS[:k]) for k in range(len(CHUNKS) + 1)]
    block_count = scales.shape[1] // 2
    spread = jnp.repeat(jnp.eye(block_count, dtype=jnp.bfloat16), width // block_count, axis=1)

    def columns(value, which, count):
        return lax.dynamic_slice_in_dim(value, which * count, count, 1)

    lat_chunks, codes_other = [], []
    partials, recons, resid_own, resid_chunks, grad_chunks, mines = [], [], [], [], [], []

    done = None
    for k in range(len(CHUNKS)):
        rows = starts[k + 1] - starts[k]
        source = latents if done is None else after(latents, done, partials[0])
        sent = lax.dynamic_slice_in_dim(source, starts[k] + core * (rows // 2), rows // 2, 0)
        got = swap(sent, "dp")
        done = got
        if partials:
            got = after(got, partials[-1])
        twin = swap(got, "lyr")
        both = jnp.where(core == 0, jnp.stack([got, twin]), jnp.stack([twin, got]))
        other = both.reshape(rows, feats)
        lat_chunks.append(jnp.concatenate([latents[starts[k] : starts[k + 1]], other]))
        partials.append(jnp.dot(lat_chunks[k], weight, preferred_element_type=jnp.float32))
        recons.append(reduce_rows(after(partials[k], *recons[: max(k - 1, 0)])))
        codes_here = after(codes, partials[k], done)[starts[k] : starts[k + 1]]
        codes_other.append(swap(columns(codes_here, 1 - half, width), "dp"))

    scales_here = after(scales, partials[0])
    weight_here = after(weight, partials[0])
    scales_own = columns(scales_here, half, block_count)
    scales_other = swap(columns(scales_here, 1 - half, block_count), "dp")
    squares = jnp.sum(jnp.square(weight_here.astype(jnp.float32)), axis=1)
    squares = squares + swap(squares, "dp")
    row_norms = jnp.sqrt(squares + epsilon)
    offset = (0.5 * penalty) * row_norms
    bias = lax.dynamic_slice_in_dim(dec_bias, half * width, width, 1)

    def inputs_of(k):
        span = slice(starts[k], starts[k + 1])
        codes_got = codes_other[k] if k == 0 else after(codes_other[k], resid_own[k - 1])
        code_rows = jnp.concatenate([columns(codes[span], half, width), codes_got])
        scale_rows = jnp.concatenate([scales_own[span], scales_other[span]])
        wide = jnp.dot(scale_rows, spread, preferred_element_type=jnp.float32)
        return code_rows.astype(jnp.float32) * wide

    count = len(CHUNKS)
    inputs_chunks = []

    def local_resid(k, *events):
        recon = after(recons[k], *partials[k + 1 :], *events)
        block = 2 * (starts[k + 1] - starts[k]) // n_lat
        inputs_chunks.append(inputs_of(k))
        inputs = lax.dynamic_slice_in_dim(inputs_chunks[k], me * block, block, 0)
        resid_own.append((recon + bias - inputs).astype(jnp.bfloat16))
        resid_chunks.append(gather_rows(resid_own[k], me))

    local_resid(0, squares)
    for k in range(count):
        resid = resid_chunks[k]
        if k >= 1:
            resid = after(resid, mines[k - 1])
        total, terms = reduce_pair(resid, weight, offset, core)
        if k + 1 < count:
            local_resid(k + 1, terms)
            total = after(total, resid_own[k + 1])
        mine = reduce_plane(total, core, column)
        if k >= 1:
            mine = after(mine, grad_chunks[k - 1])
        mines.append(mine)
        sub = (starts[k + 1] - starts[k]) // 4
        lat_mine = lax.dynamic_slice_in_dim(latents, starts[k] + layer * sub, sub, 0)
        grad_pre = jnp.where(lat_mine > 0, mine, 0.0).astype(jnp.bfloat16)
        grad_rows, pair = gather_plane(grad_pre)
        grad_chunks.append(grad_rows)

    inputs_bf = jnp.concatenate([x.astype(jnp.bfloat16) for x in inputs_chunks])
    order = after(plane_rows(core, column), resid_own[0])
    sources = []
    for k in range(count):
        sub = (starts[k + 1] - starts[k]) // 4
        source = (order * sub)[:, None] + jnp.arange(sub)[None, :]
        sources.append(2 * starts[k] + source.reshape(-1))
    rows = jnp.arange(2 * own_rows)
    selected = (rows[:, None] == jnp.concatenate(sources)[None, :]).astype(jnp.bfloat16)
    inputs_t = transposed(inputs_bf, selected)

    lat_t, act_sum = [], 0.0
    for k in range(count):
        lat = after(lat_chunks[k], resid_own[min(max(k, 1), 2)])
        lat_t.append(transposed(lat, jnp.eye(lat.shape[0], dtype=jnp.bfloat16)))
        act_sum = act_sum + jnp.sum(lat.astype(jnp.float32), axis=0)
    factor = (penalty * act_sum / row_norms)[:, None]

    grad_dec = None
    for part, event in enumerate((total, mine)):
        pieces = [after(lat_t[0], event)] + lat_t[1:]
        grad_dec = decoder_grad(pieces, resid_chunks, factor, weight, part, 2, grad_dec)
    grad_enc, grad_bias = encoder_grad(inputs_t, grad_chunks)
    return (grad_enc, grad_dec.reshape(feats, 1, width), grad_bias)


def solution(mesh):
    in_specs = (
        P("dp", "lyr", None),
        P("dp", "lyr", None),
        P("dp", "lat"),
        P("lat", "lyr", "dp"),
        P("lyr", None),
    )
    out_specs = (P("dp", "lyr", "lat"), P("lat", "lyr", "dp"), P("lat"))
    return jax.shard_map(shards, mesh=mesh, in_specs=in_specs, out_specs=out_specs, check_vma=False)
```

```python
import functools

import jax
import jax.numpy as jnp
from jax import lax
from jax.experimental import pallas as pl
from jax.experimental.pallas import tpu as pltpu
from jax.sharding import PartitionSpec as P

penalty = 1.0
epsilon = 1e-06

CHUNKS = (3, 3, 2)
LANES = 128
TILE = 1024
GROUP = 8
VMEM_BYTES = 44 * 1024 * 1024


def swap(value, axis, bit=1):
    size = lax.axis_size(axis)
    return lax.ppermute(value, axis, [(i, i ^ bit) for i in range(size)])


def swap_split(value, first_is_dp):
    n_lyr, n_dp = lax.axis_size("lyr"), lax.axis_size("dp")
    pairs = []
    for l in range(n_lyr):
        for p in range(n_dp):
            along_dp = (l % 2 == 0) == first_is_dp
            target = (l, p ^ 1) if along_dp else (l ^ 2, p)
            pairs.append((l * n_dp + p, target[0] * n_dp + target[1]))
    return lax.ppermute(value, ("lyr", "dp"), pairs)


def reduce_rows(partial):
    return lax.psum_scatter(partial, "lat", scatter_dimension=0, tiled=True)


def gather_rows(block):
    return lax.all_gather(block, "lat", axis=0, tiled=True)


def store_rows(out_ref, value):
    groups = value.shape[1] // LANES
    value = jnp.stack([value[:, j * LANES : (j + 1) * LANES] for j in range(groups)])
    out_ref[...] = jnp.swapaxes(value, 0, 1)


def product(lefts, rights):
    left = jnp.concatenate([ref[...] for ref in lefts], axis=1)
    right = jnp.concatenate([ref[...] for ref in rights], axis=0)
    return jnp.dot(left, right, preferred_element_type=jnp.float32)


def dec_kernel(count, *refs):
    factor_ref, weight_ref = refs[:2]
    lefts, rights, out_ref = refs[2 : 2 + count], refs[2 + count : 2 + 2 * count], refs[-1]
    value = product(lefts, rights)
    store_rows(out_ref, value + factor_ref[...] * weight_ref[...].astype(jnp.float32))


def enc_kernel(count, *refs):
    rights, (out_ref, bias_ref) = refs[1 : 1 + count], refs[1 + count :]
    store_rows(out_ref, product(refs[:1], rights))

    @pl.when(pl.program_id(1) == 0)
    def _():
        total = jnp.zeros(bias_ref.shape, jnp.float32)
        for ref in rights:
            total = total + jnp.sum(ref[...].astype(jnp.float32), axis=0, keepdims=True)
        bias_ref[...] = total


def params():
    return pltpu.CompilerParams(vmem_limit_bytes=VMEM_BYTES)


def decoder_grad(lefts, pieces, factor, weight, part, parts, earlier):
    feats, width = weight.shape
    rows = sum(piece.shape[0] for piece in pieces)
    share = feats // parts
    tile, step = min(TILE, share), min(GROUP * LANES, width)
    tiles = share // tile
    operands = [factor, weight, *lefts, *pieces]
    in_specs = [
        pl.BlockSpec((tile, 1), lambda i, j: (i + part * tiles, 0)),
        pl.BlockSpec((tile, step), lambda i, j: (i + part * tiles, j)),
    ]
    for left in lefts:
        in_specs.append(pl.BlockSpec((tile, left.shape[1]), lambda i, j: (i + part * tiles, 0)))
    for piece in pieces:
        in_specs.append(pl.BlockSpec((piece.shape[0], step), lambda i, j: (0, j)))
    aliases = {}
    if earlier is not None:
        aliases = {len(operands): 0}
        operands.append(earlier)
        in_specs.append(pl.BlockSpec(memory_space=pl.ANY))
    return pl.pallas_call(
        functools.partial(dec_kernel, len(pieces)),
        grid=(tiles, width // step),
        in_specs=in_specs,
        out_specs=pl.BlockSpec(
            (tile, step // LANES, LANES), lambda i, j: (i + part * tiles, j, 0)
        ),
        out_shape=jax.ShapeDtypeStruct((feats, width // LANES, LANES), jnp.float32),
        input_output_aliases=aliases,
        compiler_params=params(),
        cost_estimate=pl.CostEstimate(
            flops=2 * rows * share * width,
            bytes_accessed=share * width * 6 + rows * (share + width) * 2,
            transcendentals=0,
        ),
    )(*operands)


def encoder_grad(inputs_t, pieces):
    width, rows = inputs_t.shape
    feats = pieces[0].shape[1]
    tile, step = min(TILE, width), min(GROUP * LANES, feats)
    out, bias = pl.pallas_call(
        functools.partial(enc_kernel, len(pieces)),
        grid=(feats // step, width // tile),
        in_specs=[pl.BlockSpec((tile, rows), lambda j, i: (i, 0))]
        + [pl.BlockSpec((piece.shape[0], step), lambda j, i: (0, j)) for piece in pieces],
        out_specs=[
            pl.BlockSpec((tile, step // LANES, LANES), lambda j, i: (i, j, 0)),
            pl.BlockSpec((1, step), lambda j, i: (0, j)),
        ],
        out_shape=[
            jax.ShapeDtypeStruct((width, feats // LANES, LANES), jnp.float32),
            jax.ShapeDtypeStruct((1, feats), jnp.float32),
        ],
        compiler_params=params(),
        cost_estimate=pl.CostEstimate(
            flops=2 * rows * feats * width,
            bytes_accessed=feats * width * 4 + rows * (feats + width) * 2,
            transcendentals=0,
        ),
    )(inputs_t, *pieces)
    return out.reshape(width, 1, feats), bias.reshape(feats)


def after(value, *events):
    return lax.optimization_barrier((value,) + events)[0]


def transposed(value, selected):
    return lax.dot_general(
        value, selected, (((0,), (0,)), ((), ())), preferred_element_type=jnp.float32
    ).astype(jnp.bfloat16)


def reduce_pair(resid, weight, offset, core):
    sub, feats = resid.shape[0] // 8, weight.shape[0]
    terms = lax.dot_general(
        resid, weight, (((1,), (1,)), ((), ())), preferred_element_type=jnp.float32
    )
    blocks = (terms + offset[None, :]).reshape(2, 2, 2, sub, feats)
    to_send = lax.dynamic_index_in_dim(blocks, 1 - core, 2, keepdims=False)
    to_keep = lax.dynamic_index_in_dim(blocks, core, 2, keepdims=False)
    return (to_keep + swap(to_send, "lyr")).reshape(4, sub, feats), to_send


def reduce_plane(total, core, column):
    def pick(dp_other, column_other):
        index = 2 * dp_other + jnp.where(column_other == 1, 1 - column, column)
        return lax.dynamic_index_in_dim(total, index, 0, keepdims=False)

    first_dp, first_column = jnp.where(core == 0, 0, 1), jnp.where(core == 0, 1, 0)
    second_dp, second_column = first_column, first_dp
    got = swap_split(jnp.stack([pick(first_dp, first_column), pick(1, 1)]), False)
    mine = pick(0, 0) + got[0]
    later = pick(second_dp, second_column) + got[1]
    return mine + swap_split(later, True)


def gather_plane(mine):
    pair = jnp.stack([mine, swap_split(mine, True)])
    twin_pair = swap(pair, "lyr")
    got = swap_split(pair, False)
    twin_got = swap(got, "lyr")
    rows = jnp.concatenate([pair, got, twin_pair, twin_got])
    return rows.reshape(-1, mine.shape[1])


def plane_rows(core, column):
    order = []
    for c in (core, 1 - core):
        across, beside = 4 + 2 * column + c, 2 * (1 - column) + c
        order += [
            2 * column + c,
            jnp.where(c == 0, across, beside),
            jnp.where(c == 0, beside, across),
            4 + 2 * (1 - column) + c,
        ]
    return jnp.stack(order)


def shards(act_codes, act_scales, latents, dec_weight, dec_bias):
    me = lax.axis_index("lat")
    layer, half = lax.axis_index("lyr"), lax.axis_index("dp")
    core, column = layer % 2, layer // 2
    n_lat = lax.axis_size("lat")
    weight = dec_weight[:, 0, :]
    codes, scales = act_codes[:, 0, :], act_scales[:, 0, :]
    feats, width = weight.shape
    own_rows = latents.shape[0]
    unit = own_rows // sum(CHUNKS)
    starts = [unit * sum(CHUNKS[:k]) for k in range(len(CHUNKS) + 1)]
    block_count = scales.shape[1] // 2
    spread = jnp.repeat(jnp.eye(block_count, dtype=jnp.bfloat16), width // block_count, axis=1)

    def columns(value, which, count):
        return lax.dynamic_slice_in_dim(value, which * count, count, 1)

    lat_chunks, codes_other = [], []
    partials, recons, resid_own, resid_chunks, grad_chunks, mines = [], [], [], [], [], []

    done = None
    for k in range(len(CHUNKS)):
        rows = starts[k + 1] - starts[k]
        source = latents if done is None else after(latents, done, partials[0])
        sent = lax.dynamic_slice_in_dim(source, starts[k] + core * (rows // 2), rows // 2, 0)
        got = swap(sent, "dp")
        done = got
        if partials:
            got = after(got, partials[-1])
        twin = swap(got, "lyr")
        both = jnp.where(core == 0, jnp.stack([got, twin]), jnp.stack([twin, got]))
        other = both.reshape(rows, feats)
        lat_chunks.append(jnp.concatenate([latents[starts[k] : starts[k + 1]], other]))
        partials.append(jnp.dot(lat_chunks[k], weight, preferred_element_type=jnp.float32))
        recons.append(reduce_rows(after(partials[k], *recons[: max(k - 1, 0)])))
        codes_here = after(codes, partials[k], done)[starts[k] : starts[k + 1]]
        codes_other.append(swap(columns(codes_here, 1 - half, width), "dp"))

    scales_here = after(scales, partials[0])
    weight_here = after(weight, partials[0])
    scales_own = columns(scales_here, half, block_count)
    scales_other = swap(columns(scales_here, 1 - half, block_count), "dp")
    squares = jnp.sum(jnp.square(weight_here.astype(jnp.float32)), axis=1)
    squares = squares + swap(squares, "dp")
    row_norms = jnp.sqrt(squares + epsilon)
    offset = (0.5 * penalty) * row_norms
    bias = lax.dynamic_slice_in_dim(dec_bias, half * width, width, 1)

    def inputs_of(k):
        span = slice(starts[k], starts[k + 1])
        codes_got = codes_other[k] if k == 0 else after(codes_other[k], resid_own[k - 1])
        code_rows = jnp.concatenate([columns(codes[span], half, width), codes_got])
        scale_rows = jnp.concatenate([scales_own[span], scales_other[span]])
        wide = jnp.dot(scale_rows, spread, preferred_element_type=jnp.float32)
        return code_rows.astype(jnp.float32) * wide

    count = len(CHUNKS)
    inputs_chunks = []

    def local_resid(k, *events):
        recon = after(recons[k], *partials[k + 1 :], *events)
        block = 2 * (starts[k + 1] - starts[k]) // n_lat
        inputs_chunks.append(inputs_of(k))
        inputs = lax.dynamic_slice_in_dim(inputs_chunks[k], me * block, block, 0)
        resid_own.append((recon + bias - inputs).astype(jnp.bfloat16))
        resid_chunks.append(gather_rows(resid_own[k]))

    local_resid(0, squares)
    def finish(k, total):
        mine = reduce_plane(total, core, column)
        mines.append(mine)
        sub = (starts[k + 1] - starts[k]) // 4
        lat_mine = lax.dynamic_slice_in_dim(latents, starts[k] + layer * sub, sub, 0)
        grad_pre = jnp.where(lat_mine > 0, mine, 0.0).astype(jnp.bfloat16)
        grad_chunks.append(gather_plane(grad_pre))

    waiting = None
    for k in range(count):
        total, terms = reduce_pair(resid_chunks[k], weight, offset, core)
        if waiting is not None:
            finish(k - 1, after(waiting, terms if k < count - 1 else resid_own[k]))
        waiting = total
        if k + 1 < count:
            local_resid(k + 1, terms, *mines[k - 1 : k])
    finish(count - 1, total)
    mine = mines[-1]

    inputs_bf = jnp.concatenate([x.astype(jnp.bfloat16) for x in inputs_chunks])
    order = after(plane_rows(core, column), resid_own[0])
    sources = []
    for k in range(count):
        sub = (starts[k + 1] - starts[k]) // 4
        source = (order * sub)[:, None] + jnp.arange(sub)[None, :]
        sources.append(2 * starts[k] + source.reshape(-1))
    rows = jnp.arange(2 * own_rows)
    selected = (rows[:, None] == jnp.concatenate(sources)[None, :]).astype(jnp.bfloat16)
    inputs_t = transposed(inputs_bf, selected)

    lat_t, act_sum = [], 0.0
    for k in range(count):
        lat = after(lat_chunks[k], resid_own[min(max(k, 1), 2)])
        lat_t.append(transposed(lat, jnp.eye(lat.shape[0], dtype=jnp.bfloat16)))
        act_sum = act_sum + jnp.sum(lat.astype(jnp.float32), axis=0)
    factor = (penalty * act_sum / row_norms)[:, None]

    grad_dec = None
    for part, event in enumerate((total, mine)):
        pieces = [after(lat_t[0], event)] + lat_t[1:]
        grad_dec = decoder_grad(pieces, resid_chunks, factor, weight, part, 2, grad_dec)
    grad_enc, grad_bias = encoder_grad(inputs_t, grad_chunks)
    return (grad_enc, grad_dec.reshape(feats, 1, width), grad_bias)


def solution(mesh):
    in_specs = (
        P("dp", "lyr", None),
        P("dp", "lyr", None),
        P("dp", "lat"),
        P("lat", "lyr", "dp"),
        P("lyr", None),
    )
    out_specs = (P("dp", "lyr", "lat"), P("lat", "lyr", "dp"), P("lat"))
    return jax.shard_map(shards, mesh=mesh, in_specs=in_specs, out_specs=out_specs, check_vma=False)
```
